32 devices in a mesh: grp: 8 (over z, x), intra: 4 (over y, core).
Axes of the slice: x: 2, y: 2, z: 4, core: 2. Of those that a mesh axis runs over, the one named last changes fastest.
Arguments:
- normed: bfloat16 [4096, 4096], P(('grp', 'intra')), may hold values from -6 to 6
- cotangent: bfloat16 [4096, 1024], P(('grp', 'intra')), may hold values from -0.09375 to 0.09375
- norm_gain: float32 [4096], replicated, may hold values from 0.25 to 4
- weights: bfloat16 [4096, 1024], P('intra'), may hold values from -6 to 6
- row_state: float32 [8, 4, 86, 16], P('grp', 'intra'), may hold values from 0.05 to 20
- col_state: float32 [8, 128], replicated, may hold values from 0.3 to 10
- owner_table: int32 [512, 1], replicated, may hold values from 0 to 7; in each aligned block of 512 rows (0 to 511, 512 to 1023, ...) at most 86 rows name the same one
Outputs:
- new_weights: bfloat16 [4096, 1024], P('intra')
- row_moments: float32 [8, 4, 86, 16], P('grp', 'intra')
- col_moments: float32 [8, 128], replicated
The draws below stay inside these ranges and needn't reach their ends.
Inputs may be any that keep to these rules, and one draw needn't show every extreme that they name: `owner_table`: each group owns at most 86 units, some group exactly 86, and every group owns at least one.
All inputs are finite; a program needn't handle non-finite values.
Results may differ from the reference program's by a relative error of at most 0.013.
Values may be sent and summed in bfloat16 or wider, within the bound.
A program may use at most 64 MiB of HBM per device.

```python
import math
import jax
import jax.numpy as jnp
import numpy as np
from jax import lax

D = 4096
HD = 128
NT = 8
TOK_DEV = 128
TOKENS = 4096
UR = 16
NB = 64
NU = 512
CAP = 86
N_GRP = 8
N_INTRA = 4


def with_spikes(values, own_key, source, target, shards_of, factor):
    owner, partner = [(jnp.arange(values.shape[position]) // (values.shape[position] // shards_of)).reshape([-1 if axis == position else 1 for axis in range(values.ndim)]) for position in (source, target)]
    chosen = jax.random.permutation(own_key, shards_of)[partner]
    strong = (owner == chosen) | (owner == (partner + shards_of // 2) % shards_of)
    return jnp.where(strong, factor * values, values)


def levels(stream_key, shape, split, low, largest):
    level = 1.0
    for axis_at, shards_of in split:
        steps = jax.random.uniform(jax.random.fold_in(jax.random.fold_in(stream_key, 6), axis_at), (shards_of,), jnp.float32, low / len(split), largest / len(split))
        level = level * jnp.repeat(jnp.exp(steps), shape[axis_at] // shards_of).reshape((-1,) + (1,) * (len(shape) - 1 - axis_at))
    return level


def assign_block(own_key, own, number, rows, number_of, top, limit, lean):
    order = jax.random.permutation(own_key, number_of)
    crowded, usual = portions_of(number_of, rows * top, limit, lean, True), portions_of(number_of, rows * top, limit, lean, False)
    places = jnp.arange(number_of)

    def named(sizes, rotation):
        used = int((sizes > 0).sum())
        fixed = max(1, used // 4)
        moved = fixed + (places - fixed + rotation * (used - fixed)) % max(1, number_of - fixed)
        return jnp.zeros((number_of,), jnp.int32).at[order[jnp.where(places < fixed, places, moved)]].set(jnp.asarray(sizes, jnp.int32))

    sizes = jnp.where(number % 4 == 0, named(crowded, number // 4), named(usual, number - number // 4 - 1))
    mixed = jax.random.permutation(jax.random.fold_in(own, 3), number_of)
    donor, taker = mixed[0:number_of // 2 * 2:2], mixed[1:number_of // 2 * 2:2]
    margin = jnp.minimum(sizes[donor] - 1, limit - sizes[taker]) // 2
    margin = jnp.where((donor == order[0]) | (taker == order[0]) | (sizes[taker] == 0), 0, jnp.maximum(margin, 0))
    moved = jax.random.randint(jax.random.fold_in(own, 4), (number_of // 2,), 0, 1 << 20) % (margin + 1)
    sizes = sizes.at[donor].add(-moved).at[taker].add(moved)
    members = jnp.searchsorted(jnp.cumsum(sizes), jnp.arange(rows * top), side="right").astype(jnp.int32)
    table = members.reshape(top, rows).T
    table = table[jax.random.permutation(jax.random.fold_in(own, 1), rows)]
    rotation = jax.random.randint(jax.random.fold_in(own, 2), (rows, 1), 0, top)
    return jnp.take_along_axis(table, (jnp.arange(top)[None, :] + rotation) % top, axis=1)


def portions_of(count, total, bound, skew, full):
    weights = [(1 << 20) // math.isqrt(standing ** skew) + 1 for standing in range(1, count + 1)]
    largest = bound if full else min(bound, max(-(-total // count), total * weights[0] // sum(weights)))
    least = 1 if total - largest >= count - 1 else 0
    counts, rest = [largest] + [least] * (count - 1), total - largest - least * (count - 1)
    while rest > 0:
        movable = [i for i in range(1, count) if counts[i] < largest] or [i for i in range(1, count) if counts[i] < bound]
        whole, budget = sum([weights[i] for i in movable]), rest
        for i in movable:
            addition = min(bound - counts[i], max(1, budget * weights[i] // whole), rest)
            counts[i] = counts[i] + addition
            rest = rest - addition
    return np.array(counts)


def scatter_about(own_key, extent, scale, reach, cuts=(), held_as=jnp.bfloat16):
    array = jax.random.normal(own_key, extent, jnp.float32) * scale
    if len(cuts) > 0:
        array = levels(own_key, extent, cuts, -0.22, 0.18) * array
    return jnp.clip(array, min=-reach, max=reach).astype(held_as)


def noise_with(rng, dims, deviation, most, pieces, heavy, kind=jnp.bfloat16):
    result = deviation * jax.random.normal(rng, dims, jnp.float32)
    if pieces:
        result = result * levels(rng, dims, pieces, -0.22, 0.18)
    return jnp.clip(with_spikes(result, jax.random.fold_in(rng, 3), *heavy), -most, most).astype(kind)


def setup_inputs(seed: int = 0) -> dict:
    arg_keys = jax.random.split(jax.random.key(seed), 8)
    normed = noise_with(arg_keys[0], (TOKENS, D), 1.0, 6.0, ((0, 32),), (0, 1, 32, 2.75))
    cotangent = scatter_about(arg_keys[1], (TOKENS, NT * HD), TOKENS ** -0.5, 0.09375, ((0, 32),))
    norm_gain = jnp.clip(jnp.exp(jax.random.uniform(arg_keys[2], (D,), jnp.float32, math.log(0.25), math.log(4.0))), 0.25, 4.0)
    weights = scatter_about(arg_keys[3], (D, NT * HD), 1.0, 6.0, ((0, 4),))
    row_state = jnp.clip(jnp.exp(math.log(20.0) - 5.9914645 * jax.random.uniform(arg_keys[4], (N_GRP, N_INTRA, CAP, UR), jnp.float32) ** levels(arg_keys[4], (N_GRP, N_INTRA, CAP, UR), ((0, 8), (1, 4)), -0.2, 0.2)), 0.05, 20.0)
    col_state = jnp.clip(jnp.exp(jax.random.uniform(arg_keys[5], (NT, HD), jnp.float32, math.log(0.3), math.log(10.0))), 0.3, 10.0)
    owner_table_keys = jax.random.split(jax.random.fold_in(arg_keys[6], 1), NU // NU)
    owner_table_turns = jax.random.permutation(jax.random.fold_in(arg_keys[6], 3), NU // NU)
    owner_table = jax.vmap(lambda own, number: assign_block(jax.random.fold_in(arg_keys[6], 2), own, number, NU, N_GRP, 1, CAP, 2))(owner_table_keys, owner_table_turns).reshape((NU, 1))
    return dict(normed=normed, cotangent=cotangent, norm_gain=norm_gain, weights=weights, row_state=row_state, col_state=col_state, owner_table=owner_table)


decay_rate = 0.8
step_size = 0.5
epsilon = 1e-06

def slots_of(owner_flat):
    onehot = (owner_flat[:, None] == jnp.arange(N_GRP, dtype=jnp.int32)[None, :]).astype(jnp.int32)
    before = jnp.cumsum(onehot, axis=0) - onehot
    return lax.optimization_barrier(jnp.sum(before * onehot, axis=1)).astype(jnp.int32)

def reference(normed, cotangent, norm_gain, weights, row_state, col_state, owner_table):
    scaled = (normed * norm_gain[None, :]).astype(jnp.bfloat16)
    width = NT * HD
    acts = scaled.reshape(N_GRP, N_INTRA, TOK_DEV, D)
    grads = cotangent.reshape(N_GRP, N_INTRA, TOK_DEV, width)

    def member(total, pair):
        left, right = pair
        term = jnp.dot(left.T, right, preferred_element_type=jnp.float32).astype(jnp.bfloat16)
        term = lax.optimization_barrier(term)
        return (total + term.astype(jnp.float32), None)

    def group(total, pair):
        inner, _ = lax.scan(member, jnp.zeros((D, width), jnp.float32), pair)
        return (total + inner, None)
    grad, _ = lax.scan(group, jnp.zeros((D, width), jnp.float32), (acts, grads))
    cube_grad = grad.reshape(D, NT, HD)
    squares = cube_grad * cube_grad
    row_mean = lax.optimization_barrier(jnp.mean(squares, axis=2)) + epsilon
    col_mean = lax.optimization_barrier(jnp.mean(squares, axis=0)) + epsilon
    owner_flat = owner_table[:, 0].astype(jnp.int32)
    slot = slots_of(owner_flat)
    prev_units = row_state[owner_flat, :, slot, :]
    prev_rows = prev_units.reshape(NT, NB, N_INTRA, UR).transpose(0, 2, 1, 3).reshape(NT, D).T
    row_new = decay_rate * prev_rows + (1.0 - decay_rate) * row_mean
    row_avg = lax.optimization_barrier(jnp.mean(row_new, axis=0))
    col_new = decay_rate * col_state + (1.0 - decay_rate) * col_mean
    variance = row_new[:, :, None] * col_new[None, :, :] / row_avg[None, :, None]
    updated = weights.reshape(D, NT, HD).astype(jnp.float32) - step_size * cube_grad / jnp.sqrt(variance)
    new_weights = updated.reshape(D, width).astype(jnp.bfloat16)
    row_units = row_new.T.reshape(NT, N_INTRA, NB, UR).transpose(0, 2, 1, 3).reshape(NU, N_INTRA, UR)
    row_moments = jnp.zeros((N_GRP, N_INTRA, CAP, UR), jnp.float32).at[owner_flat, :, slot, :].set(row_units)
    return (new_weights, row_moments, col_new)
```

```python
import functools

import jax
import jax.numpy as jnp
from jax import lax
from jax.experimental import pallas as pl
from jax.experimental.pallas import tpu as pltpu
from jax.sharding import PartitionSpec as P

decay_rate = 0.8
step_size = 0.5
epsilon = 1e-06

MESH = pl.DeviceIdType.MESH
HIGH = lax.Precision.HIGHEST
CHUNKS = 4


def to_units(block, blocks, unit_rows, tensors, head):
    return (
        block.reshape(blocks, unit_rows, tensors, head)
        .transpose(2, 0, 1, 3)
        .reshape(tensors * blocks, unit_rows * head)
    )


def from_units(units, blocks, unit_rows, tensors, head):
    return (
        units.reshape(tensors, blocks, unit_rows, head)
        .transpose(1, 2, 0, 3)
        .reshape(blocks * unit_rows, tensors * head)
    )


def pick(hot, rows):
    return jnp.dot(hot.astype(jnp.bfloat16), rows, preferred_element_type=jnp.float32)


def general(normed, cotangent, norm_gain, weights, row_state, col_state, owner_table):
    groups = lax.axis_size("grp")
    members = lax.axis_size("intra")
    d_model = normed.shape[1]
    tokens_here = cotangent.shape[0]
    width = cotangent.shape[1]
    tensors = col_state.shape[0]
    head = col_state.shape[1]
    capacity = row_state.shape[2]
    unit_rows = row_state.shape[3]
    slab_rows = weights.shape[0]
    blocks = slab_rows // unit_rows
    unit_count = tensors * blocks
    scaled = (normed * norm_gain[None, :]).astype(jnp.bfloat16)
    columns = lax.all_to_all(scaled, "intra", split_axis=1, concat_axis=0, tiled=True)
    peer_grads = lax.all_gather(cotangent, "intra", axis=0, tiled=True)

    def add_term(total, pair):
        left, right = pair
        term = lax.dot_general(
            left, right, (((0,), (0,)), ((), ())), preferred_element_type=jnp.float32
        )
        return (total + term, None)

    slab, _ = lax.scan(
        add_term,
        jnp.zeros((slab_rows, width), jnp.float32),
        (
            columns.reshape(members, tokens_here, slab_rows),
            peer_grads.reshape(members, tokens_here, width),
        ),
    )
    owner_flat = owner_table[:, 0]
    owner_hot = owner_flat[:, None] == jnp.arange(groups, dtype=jnp.int32)[None, :]
    ids = jnp.arange(unit_count, dtype=jnp.int32)
    earlier = (owner_flat[:, None] == owner_flat[None, :]) & (ids[None, :] < ids[:, None])
    slot = jnp.sum(earlier.astype(jnp.int32), axis=1)
    place = owner_flat * capacity + slot
    hot = place[:, None] == jnp.arange(groups * capacity, dtype=jnp.int32)[None, :]
    my_group = lax.axis_index("grp")
    my_place = my_group * capacity + jnp.arange(capacity, dtype=jnp.int32)
    my_hot = my_place[:, None] == place[None, :]
    valid = jnp.any(my_hot, axis=1)
    weight_units = to_units(weights, blocks, unit_rows, tensors, head)
    grad_units = to_units(slab, blocks, unit_rows, tensors, head).astype(jnp.bfloat16)
    outgoing = pick(hot.T, grad_units).reshape(groups, capacity, unit_rows, head)
    incoming = lax.all_to_all(
        outgoing.astype(jnp.bfloat16), "grp", split_axis=0, concat_axis=0, tiled=True
    ).astype(jnp.float32)
    grad_own = jnp.sum(incoming, axis=0)
    own_weights = pick(my_hot, weight_units).reshape(capacity, unit_rows, head)
    unit_hot = (
        (ids // blocks)[:, None] == jnp.arange(tensors, dtype=jnp.int32)[None, :]
    ).astype(jnp.bfloat16)
    tensor_hot = pick(my_hot, unit_hot)
    squares = grad_own * grad_own
    row_mean = jnp.mean(squares, axis=2) + epsilon
    row_new = jnp.where(
        valid[:, None], decay_rate * row_state[0, 0] + (1.0 - decay_rate) * row_mean, 0.0
    )
    col_part = jnp.einsum("st,srh->th", tensor_hot, squares, precision=HIGH)
    row_part = jnp.einsum("st,sr->t", tensor_hot, row_new, precision=HIGH)
    col_total, row_total = lax.psum((col_part, row_part), ("grp", "intra"))
    col_new = decay_rate * col_state + (1.0 - decay_rate) * (col_total / d_model + epsilon)
    row_avg = row_total / d_model
    col_slot = jnp.dot(tensor_hot, col_new, precision=HIGH)
    avg_slot = jnp.where(valid, jnp.dot(tensor_hot, row_avg, precision=HIGH), 1.0)
    variance = row_new[:, :, None] * col_slot[:, None, :] / avg_slot[:, None, None]
    variance = jnp.where(valid[:, None, None], variance, 1.0)
    updated = (own_weights - step_size * grad_own / jnp.sqrt(variance)).astype(jnp.bfloat16)
    collected = lax.all_gather(updated, "grp", axis=0, tiled=True)
    mine = pick(hot, collected.reshape(groups * capacity, unit_rows * head)).astype(jnp.bfloat16)
    new_weights = from_units(mine, blocks, unit_rows, tensors, head)
    return (new_weights, row_new[None, None], col_new)


def iota(shape, axis):
    return lax.broadcasted_iota(jnp.int32, shape, axis)


def kernel(
    d_model,
    normed,
    cot,
    gain,
    weights,
    state,
    col_state,
    owner,
    out,
    row_out,
    col_out,
    x_all,
    c_all,
    w_own,
    st_all,
    slots,
    owners,
    prev,
    part,
    x_recv,
    z_send,
    z_recv,
    grad,
    rows_new,
    stat,
    note,
    new_own,
    local_sem,
    cs,
    cr,
    xs,
    xr,
    ss,
    sr,
    ps,
    pr,
    zs,
    zr,
    ts,
    tr,
    ns,
    nr,
    us,
    ur,
    fs,
    fr,
):
    groups = lax.axis_size("grp")
    members = lax.axis_size("intra")
    g = lax.axis_index("grp")
    i = lax.axis_index("intra")
    z, x = g // 2, g % 2
    zn = groups // 2
    tokens = cot.shape[0]
    slab = grad.shape[0]
    head = grad.shape[1]
    capacity, unit_rows = state.shape[1], state.shape[0]
    units = owner.shape[1]
    blocks = slab // unit_rows
    step = slab // CHUNKS
    other_core = i // 2 * 2 + (1 - i % 2)
    other_y = (1 - i // 2) * 2 + i % 2
    other_x = z * 2 + (1 - x)

    def grp_peer(d):
        return lax.rem(g + d, groups)

    def z_peer(d):
        return lax.rem(z + d, zn) * 2 + x

    def intra_peer(d):
        return lax.rem(i + d, members)

    def remote(src, dst, send, recv, to):
        return pltpu.make_async_remote_copy(
            src_ref=src, dst_ref=dst, send_sem=send, recv_sem=recv, device_id=to, device_id_type=MESH
        )

    local = [
        pltpu.make_async_copy(cot, c_all.at[i], local_sem.at[0]),
        pltpu.make_async_copy(
            normed.at[:, pl.ds(pl.multiple_of(i * slab, slab), slab)], x_all.at[0], local_sem.at[1]
        ),
        pltpu.make_async_copy(
            weights.at[:, pl.ds(pl.multiple_of(g * head, head), head)], w_own, local_sem.at[2]
        ),
    ]
    for copy in local:
        copy.start()

    barrier = pltpu.get_barrier_semaphore()
    for d in range(1, groups):
        pl.semaphore_signal(barrier, inc=1, device_id=(grp_peer(d), i), device_id_type=MESH)
    for d in range(1, members):
        pl.semaphore_signal(barrier, inc=1, device_id=(g, intra_peer(d)), device_id_type=MESH)
    st_all[0] = jnp.zeros_like(st_all[0])
    st_all[0, :, :capacity] = state[...]
    pl.semaphore_wait(barrier, groups + members - 2)

    cot_y = remote(cot, c_all.at[i], cs.at[0], cr.at[0], (g, other_y))
    cot_core = remote(cot, c_all.at[i], cs.at[1], cr.at[1], (g, other_core))
    cot_on = remote(c_all.at[other_y], c_all.at[other_y], cs.at[2], cr.at[2], (g, other_core))
    cot_y.start()
    cot_core.start()
    x_copies = {}
    for k in range(CHUNKS):
        for d in range(1, members):
            to = intra_peer(d)
            x_copies[k, d] = remote(
                normed.at[:, pl.ds(pl.multiple_of(to * slab + k * step, step), step)],
                x_all.at[d, :, pl.ds(k * step, step)],
                xs.at[k, d],
                xr.at[k, d],
                (g, to),
            )
            x_copies[k, d].start()
    state_copies = []
    for d in range(1, groups):
        copy = remote(st_all.at[0], st_all.at[d], ss.at[d], sr.at[d], (grp_peer(d), i))
        copy.start()
        state_copies.append(copy)

    own_row = owner[...]
    mine_col = jnp.sum(
        jnp.where(iota((units, units), 0) == iota((units, units), 1), own_row, 0).astype(jnp.float32),
        axis=1,
        keepdims=True,
    )
    same = (mine_col == own_row.astype(jnp.float32)) & (iota((units, units), 1) < iota((units, units), 0))
    slots[...] = jnp.sum(jnp.where(same, 1.0, 0.0), axis=1, keepdims=True)
    owners[...] = mine_col

    cot_y.wait_recv()
    cot_on.start()
    for copy in state_copies:
        copy.wait_recv()
    base = pl.ds(pl.multiple_of(g * blocks, blocks), blocks)
    my_owner, my_slot = owners[base, :], slots[base, :]
    lane = iota((blocks, 128), 1).astype(jnp.float32)
    old = jnp.zeros((blocks, unit_rows), jnp.float32)
    for d in range(groups):
        source = lax.rem(g + groups - d, groups).astype(jnp.float32)
        hot = jnp.where((lane == my_slot) & (my_owner == source), 1.0, 0.0)
        old = old + lax.dot_general(
            hot, st_all[d], (((1,), (1,)), ((), ())), precision=HIGH, preferred_element_type=jnp.float32
        )

    def expand():
        return jnp.where(iota((slab, blocks), 0) // unit_rows == iota((slab, blocks), 1), 1.0, 0.0)

    def diagonal():
        return iota((slab, unit_rows), 0) % unit_rows == iota((slab, unit_rows), 1)

    spread = lax.dot_general(
        expand(), old, (((1,), (0,)), ((), ())), precision=HIGH, preferred_element_type=jnp.float32
    )
    prev[...] = jnp.sum(jnp.where(diagonal(), spread, 0.0), axis=1, keepdims=True)

    for copy in local:
        copy.wait()
    cot_core.wait_recv()
    cot_on.wait_recv()

    def rows(k):
        return pl.ds(k * step, step)

    part_copies, z_copies = {}, {}

    def multiply(k):
        for d in range(1, members):
            x_copies[k, d].wait_recv()
        gains = gain[:, pl.ds(pl.multiple_of(i * slab + k * step, step), step)]
        total = jnp.zeros((step, cot.shape[1]), jnp.float32)
        for d in range(members):
            scaled = (x_all[d, :, rows(k)].astype(jnp.float32) * gains).astype(jnp.bfloat16)
            total = total + lax.dot_general(
                scaled,
                c_all[lax.rem(i + members - d, members)],
                (((0,), (0,)), ((), ())),
                preferred_element_type=jnp.float32,
            )
        total = total.astype(jnp.bfloat16)
        for t in range(groups):
            part[t // 2, t % 2, rows(k), :] = total[:, t * head : (t + 1) * head]
        part_copies[k] = remote(
            part.at[:, 1 - x, rows(k), :], x_recv.at[:, rows(k), :], ps.at[k], pr.at[k], (other_x, i)
        )
        part_copies[k].start()

    def pass_on(k):
        part_copies[k].wait_recv()
        for d in range(zn):
            to = lax.rem(z + d, zn)
            both = part[to, x, rows(k), :].astype(jnp.float32) + x_recv[to, rows(k), :].astype(jnp.float32)
            if d == 0:
                grad[rows(k), :] = both
                continue
            z_send[d, rows(k), :] = both.astype(jnp.bfloat16)
            z_copies[k, d] = remote(
                z_send.at[d, rows(k), :], z_recv.at[d, rows(k), :], zs.at[k, d], zr.at[k, d], (z_peer(d), i)
            )
            z_copies[k, d].start()

    sums = []

    def finish(k):
        total = grad[rows(k), :]
        for d in range(1, zn):
            z_copies[k, d].wait_recv()
            total = total + z_recv[d, rows(k), :].astype(jnp.float32)
        grad[rows(k), :] = total
        squares = total * total
        mean = jnp.sum(squares, axis=1, keepdims=True) / head + epsilon
        row = decay_rate * prev[rows(k), :] + (1.0 - decay_rate) * mean
        rows_new[rows(k), :] = row
        sums.append(
            (jnp.sum(squares, axis=0, keepdims=True), jnp.sum(jnp.broadcast_to(row, squares.shape), axis=0, keepdims=True))
        )

    for k in range(CHUNKS + 2):
        if k < CHUNKS:
            multiply(k)
        if 0 <= k - 1 < CHUNKS:
            pass_on(k - 1)
        if 0 <= k - 2:
            finish(k - 2)

    stat[0, 0:1, :] = sum(s[0] for s in sums)
    stat[0, 1:2, :] = sum(s[1] for s in sums)
    stat_copies = []
    for d in range(1, members):
        copy = remote(stat.at[0], stat.at[d], ts.at[d], tr.at[d], (g, intra_peer(d)))
        copy.start()
        stat_copies.append(copy)
    note[0, 0:unit_rows, 0:blocks] = lax.dot_general(
        jnp.where(diagonal(), rows_new[...], 0.0),
        expand(),
        (((0,), (0,)), ((), ())),
        precision=HIGH,
        preferred_element_type=jnp.float32,
    )
    for copy in stat_copies:
        copy.wait_recv()
    col_total = stat[0, 0:1, :]
    row_total = stat[0, 1:2, :]
    for d in range(1, members):
        col_total = col_total + stat[d, 0:1, :]
        row_total = row_total + stat[d, 1:2, :]
    col_new = decay_rate * col_state[pl.ds(g, 1), :] + (1.0 - decay_rate) * (col_total / d_model + epsilon)
    note[0, unit_rows : unit_rows + 1, :] = col_new
    col_factor = step_size * lax.rsqrt(col_new / (row_total / d_model))

    note_copies = []
    for d in range(1, groups):
        copy = remote(note.at[0], note.at[d], ns.at[d], nr.at[d], (grp_peer(d), i))
        copy.start()
        note_copies.append(copy)

    def columns(t):
        return pl.ds(pl.multiple_of(t * head, head), head)

    new_copies, forwards = {}, {}
    for k in range(CHUNKS):
        change = grad[rows(k), :] * lax.rsqrt(rows_new[rows(k), :]) * col_factor
        fresh = (w_own[rows(k), :].astype(jnp.float32) - change).astype(jnp.bfloat16)
        new_own[rows(k), :] = fresh
        out[rows(k), columns(g)] = fresh
        for d in range(1, zn):
            new_copies[k, d] = remote(
                new_own.at[rows(k), :], out.at[rows(k), columns(g)], us.at[k, d], ur.at[k, d], (z_peer(d), i)
            )
            new_copies[k, d].start()
        forwards[k, 0] = remote(
            new_own.at[rows(k), :], out.at[rows(k), columns(g)], fs.at[k, 0], fr.at[k, 0], (other_x, i)
        )
        forwards[k, 0].start()
    for k in range(CHUNKS):
        for d in range(1, zn):
            new_copies[k, d].wait_recv()
            at = columns(lax.rem(z + zn - d, zn) * 2 + x)
            forwards[k, d] = remote(
                out.at[rows(k), at], out.at[rows(k), at], fs.at[k, d], fr.at[k, d], (other_x, i)
            )
            forwards[k, d].start()

    for copy in note_copies:
        copy.wait_recv()
    got = jnp.zeros((unit_rows, 128), jnp.float32)
    me = g.astype(jnp.float32)
    for d in range(groups):
        t = lax.rem(g + groups - d, groups)
        at = pl.ds(pl.multiple_of(t * blocks, blocks), blocks)
        hot = jnp.where((lane == slots[at, :]) & (owners[at, :] == me), 1.0, 0.0)
        got = got + lax.dot_general(
            note[d, 0:unit_rows, 0:blocks],
            hot,
            (((1,), (0,)), ((), ())),
            precision=HIGH,
            preferred_element_type=jnp.float32,
        )
        col_out[pl.ds(t, 1), :] = note[d, unit_rows : unit_rows + 1, :]
    row_out[...] = got[:, :capacity]

    for k in range(CHUNKS):
        for d in range(zn):
            forwards[k, d].wait_recv()
    sent = [cot_y, cot_core, cot_on, *x_copies.values(), *state_copies, *part_copies.values()]
    sent += [*z_copies.values(), *stat_copies, *note_copies, *new_copies.values(), *forwards.values()]
    for copy in sent:
        copy.wait_send()


def fused(normed, cotangent, norm_gain, weights, row_state, col_state, owner_table):
    groups = lax.axis_size("grp")
    members = lax.axis_size("intra")
    tokens, d_model = normed.shape
    slab, width = weights.shape
    tensors, head = col_state.shape
    capacity, unit_rows = row_state.shape[2:]
    units = owner_table.shape[0]
    zn = groups // 2
    bf16, f32 = jnp.bfloat16, jnp.float32
    vmem = pl.BlockSpec(memory_space=pltpu.VMEM)
    anywhere = pl.BlockSpec(memory_space=pl.ANY)
    dma = pltpu.SemaphoreType.DMA
    note_rows = unit_rows + 8
    out, row_out, col_out = pl.pallas_call(
        functools.partial(kernel, d_model),
        out_shape=(
            jax.ShapeDtypeStruct((slab, width), bf16),
            jax.ShapeDtypeStruct((unit_rows, capacity), f32),
            jax.ShapeDtypeStruct((tensors, head), f32),
        ),
        in_specs=[anywhere, anywhere, vmem, anywhere, vmem, vmem, vmem],
        out_specs=(vmem, vmem, vmem),
        scratch_shapes=[
            pltpu.VMEM((members, tokens, slab), bf16),
            pltpu.VMEM((members, tokens, width), bf16),
            pltpu.VMEM((slab, head), bf16),
            pltpu.VMEM((groups, unit_rows, 128), f32),
            pltpu.VMEM((units, 1), f32),
            pltpu.VMEM((units, 1), f32),
            pltpu.VMEM((slab, 1), f32),
            pltpu.VMEM((zn, 2, slab, head), bf16),
            pltpu.VMEM((zn, slab, head), bf16),
            pltpu.VMEM((zn, slab, head), bf16),
            pltpu.VMEM((zn, slab, head), bf16),
            pltpu.VMEM((slab, head), f32),
            pltpu.VMEM((slab, 1), f32),
            pltpu.VMEM((members, 8, head), f32),
            pltpu.VMEM((groups, note_rows, 128), f32),
            pltpu.VMEM((slab, head), bf16),
            dma((3,)),
            dma((3,)),
            dma((3,)),
            dma((CHUNKS, members)),
            dma((CHUNKS, members)),
            dma((groups,)),
            dma((groups,)),
            dma((CHUNKS,)),
            dma((CHUNKS,)),
            dma((CHUNKS, zn)),
            dma((CHUNKS, zn)),
            dma((members,)),
            dma((members,)),
            dma((groups,)),
            dma((groups,)),
            dma((CHUNKS, zn)),
            dma((CHUNKS, zn)),
            dma((CHUNKS, zn)),
            dma((CHUNKS, zn)),
        ],
        compiler_params=pltpu.CompilerParams(
            collective_id=0, has_side_effects=True, vmem_limit_bytes=40 * 2**20
        ),
        cost_estimate=pl.CostEstimate(
            flops=2 * members * tokens * slab * width, bytes_accessed=6 * 2**20, transcendentals=0
        ),
    )(
        normed,
        cotangent,
        norm_gain.reshape(1, d_model),
        weights,
        row_state[0, 0].T,
        col_state,
        owner_table.reshape(1, units),
    )
    return (out, row_out.T[None, None], col_out)


def solution(mesh):
    placed = (
        P(("grp", "intra"), None),
        P(("grp", "intra"), None),
        P(),
        P("intra", None),
        P("grp", "intra", None, None),
        P(),
        P(),
    )
    fits = mesh.shape["grp"] == 8 and mesh.shape["intra"] == 4
    return jax.shard_map(
        fused if fits else general,
        mesh=mesh,
        in_specs=placed,
        out_specs=(P("intra", None), P("grp", "intra", None, None), P()),
        check_vma=False,
    )
```

```python
import functools

import jax
import jax.numpy as jnp
from jax import lax
from jax.experimental import pallas as pl
from jax.experimental.pallas import tpu as pltpu
from jax.sharding import PartitionSpec as P

decay_rate = 0.8
step_size = 0.5
epsilon = 1e-06

MESH = pl.DeviceIdType.MESH
HIGH = lax.Precision.HIGHEST
CHUNKS = 8


def to_units(block, blocks, unit_rows, tensors, head):
    return (
        block.reshape(blocks, unit_rows, tensors, head)
        .transpose(2, 0, 1, 3)
        .reshape(tensors * blocks, unit_rows * head)
    )


def from_units(units, blocks, unit_rows, tensors, head):
    return (
        units.reshape(tensors, blocks, unit_rows, head)
        .transpose(1, 2, 0, 3)
        .reshape(blocks * unit_rows, tensors * head)
    )


def pick(hot, rows):
    return jnp.dot(hot.astype(jnp.bfloat16), rows, preferred_element_type=jnp.float32)


def general(normed, cotangent, norm_gain, weights, row_state, col_state, owner_table):
    groups = lax.axis_size("grp")
    members = lax.axis_size("intra")
    d_model = normed.shape[1]
    tokens_here = cotangent.shape[0]
    width = cotangent.shape[1]
    tensors = col_state.shape[0]
    head = col_state.shape[1]
    capacity = row_state.shape[2]
    unit_rows = row_state.shape[3]
    slab_rows = weights.shape[0]
    blocks = slab_rows // unit_rows
    unit_count = tensors * blocks
    scaled = (normed * norm_gain[None, :]).astype(jnp.bfloat16)
    columns = lax.all_to_all(scaled, "intra", split_axis=1, concat_axis=0, tiled=True)
    peer_grads = lax.all_gather(cotangent, "intra", axis=0, tiled=True)

    def add_term(total, pair):
        left, right = pair
        term = lax.dot_general(
            left, right, (((0,), (0,)), ((), ())), preferred_element_type=jnp.float32
        )
        return (total + term, None)

    slab, _ = lax.scan(
        add_term,
        jnp.zeros((slab_rows, width), jnp.float32),
        (
            columns.reshape(members, tokens_here, slab_rows),
            peer_grads.reshape(members, tokens_here, width),
        ),
    )
    owner_flat = owner_table[:, 0]
    owner_hot = owner_flat[:, None] == jnp.arange(groups, dtype=jnp.int32)[None, :]
    ids = jnp.arange(unit_count, dtype=jnp.int32)
    earlier = (owner_flat[:, None] == owner_flat[None, :]) & (ids[None, :] < ids[:, None])
    slot = jnp.sum(earlier.astype(jnp.int32), axis=1)
    place = owner_flat * capacity + slot
    hot = place[:, None] == jnp.arange(groups * capacity, dtype=jnp.int32)[None, :]
    my_group = lax.axis_index("grp")
    my_place = my_group * capacity + jnp.arange(capacity, dtype=jnp.int32)
    my_hot = my_place[:, None] == place[None, :]
    valid = jnp.any(my_hot, axis=1)
    weight_units = to_units(weights, blocks, unit_rows, tensors, head)
    grad_units = to_units(slab, blocks, unit_rows, tensors, head).astype(jnp.bfloat16)
    outgoing = pick(hot.T, grad_units).reshape(groups, capacity, unit_rows, head)
    incoming = lax.all_to_all(
        outgoing.astype(jnp.bfloat16), "grp", split_axis=0, concat_axis=0, tiled=True
    ).astype(jnp.float32)
    grad_own = jnp.sum(incoming, axis=0)
    own_weights = pick(my_hot, weight_units).reshape(capacity, unit_rows, head)
    unit_hot = (
        (ids // blocks)[:, None] == jnp.arange(tensors, dtype=jnp.int32)[None, :]
    ).astype(jnp.bfloat16)
    tensor_hot = pick(my_hot, unit_hot)
    squares = grad_own * grad_own
    row_mean = jnp.mean(squares, axis=2) + epsilon
    row_new = jnp.where(
        valid[:, None], decay_rate * row_state[0, 0] + (1.0 - decay_rate) * row_mean, 0.0
    )
    col_part = jnp.einsum("st,srh->th", tensor_hot, squares, precision=HIGH)
    row_part = jnp.einsum("st,sr->t", tensor_hot, row_new, precision=HIGH)
    col_total, row_total = lax.psum((col_part, row_part), ("grp", "intra"))
    col_new = decay_rate * col_state + (1.0 - decay_rate) * (col_total / d_model + epsilon)
    row_avg = row_total / d_model
    col_slot = jnp.dot(tensor_hot, col_new, precision=HIGH)
    avg_slot = jnp.where(valid, jnp.dot(tensor_hot, row_avg, precision=HIGH), 1.0)
    variance = row_new[:, :, None] * col_slot[:, None, :] / avg_slot[:, None, None]
    variance = jnp.where(valid[:, None, None], variance, 1.0)
    updated = (own_weights - step_size * grad_own / jnp.sqrt(variance)).astype(jnp.bfloat16)
    collected = lax.all_gather(updated, "grp", axis=0, tiled=True)
    mine = pick(hot, collected.reshape(groups * capacity, unit_rows * head)).astype(jnp.bfloat16)
    new_weights = from_units(mine, blocks, unit_rows, tensors, head)
    return (new_weights, row_new[None, None], col_new)


def iota(shape, axis):
    return lax.broadcasted_iota(jnp.int32, shape, axis)


def kernel(
    d_model,
    normed,
    cot,
    gain_in,
    weights,
    state_in,
    col_in,
    owner_in,
    out,
    row_out,
    col_out,
    gain,
    state,
    col_state,
    owner,
    x_all,
    c_all,
    w_all,
    st_all,
    slots,
    owners,
    old,
    factor,
    part,
    x_recv,
    z_send,
    z_recv,
    grad,
    rows_new,
    gathered,
    stat,
    note,
    local_sem,
    cs,
    cr,
    xs,
    xr,
    ss,
    sr,
    ps,
    pr,
    zs,
    zr,
    ts,
    tr,
    ns,
    nr,
    us,
    ur,
    fs,
    fr,
):
    groups = lax.axis_size("grp")
    members = lax.axis_size("intra")
    g = lax.axis_index("grp")
    i = lax.axis_index("intra")
    z, x = g // 2, g % 2
    zn = groups // 2
    slab = grad.shape[0]
    head = grad.shape[1]
    capacity, unit_rows = state.shape[1], state.shape[0]
    units = owner.shape[1]
    blocks = slab // unit_rows
    step = slab // CHUNKS
    other_core = i // 2 * 2 + (1 - i % 2)
    other_y = (1 - i // 2) * 2 + i % 2
    other_x = z * 2 + (1 - x)

    def grp_peer(d):
        return lax.rem(g + d, groups)

    def z_peer(d):
        return lax.rem(z + d, zn) * 2 + x

    def intra_peer(d):
        return lax.rem(i + d, members)

    def remote(src, dst, send, recv, to):
        return pltpu.make_async_remote_copy(
            src_ref=src, dst_ref=dst, send_sem=send, recv_sem=recv, device_id=to, device_id_type=MESH
        )

    barrier = pltpu.get_barrier_semaphore()
    for d in range(1, groups):
        pl.semaphore_signal(barrier, inc=1, device_id=(grp_peer(d), i), device_id_type=MESH)
    for d in range(1, members):
        pl.semaphore_signal(barrier, inc=1, device_id=(g, intra_peer(d)), device_id_type=MESH)

    slab_at = pl.ds(pl.multiple_of(i * slab, slab), slab)
    local = [
        pltpu.make_async_copy(state_in, state, local_sem.at[0]),
        pltpu.make_async_copy(owner_in, owner, local_sem.at[1]),
        pltpu.make_async_copy(cot, c_all.at[i], local_sem.at[2]),
        pltpu.make_async_copy(normed.at[:, slab_at], x_all.at[0], local_sem.at[3]),
        pltpu.make_async_copy(gain_in.at[:, slab_at], gain, local_sem.at[4]),
        pltpu.make_async_copy(col_in, col_state, local_sem.at[5]),
        pltpu.make_async_copy(weights, w_all, local_sem.at[6]),
    ]
    for copy in local:
        copy.start()
    st_all[g] = jnp.zeros_like(st_all[0])
    local[0].wait()
    st_all[g, :, :capacity] = state[...]
    pl.semaphore_wait(barrier, groups + members - 2)

    cot_y = remote(cot, c_all.at[i], cs.at[0], cr.at[0], (g, other_y))
    cot_core = remote(cot, c_all.at[i], cs.at[1], cr.at[1], (g, other_core))
    cot_on = remote(c_all.at[other_y], c_all.at[other_y], cs.at[2], cr.at[2], (g, other_core))
    cot_y.start()
    cot_core.start()
    x_copies = {}
    for k in range(CHUNKS):
        for d in range(1, members):
            to = intra_peer(d)
            x_copies[k, d] = remote(
                normed.at[:, pl.ds(pl.multiple_of(to * slab + k * step, step), step)],
                x_all.at[d, :, pl.ds(k * step, step)],
                xs.at[k, d],
                xr.at[k, d],
                (g, to),
            )
            x_copies[k, d].start()
    state_copies = []
    for d in range(1, groups):
        copy = remote(st_all.at[g], st_all.at[g], ss.at[d], sr.at[d], (grp_peer(d), i))
        copy.start()
        state_copies.append(copy)

    local[1].wait()
    own_row = owner[...].astype(jnp.float32)
    mine_col = jnp.sum(
        jnp.where(iota((units, units), 0) == iota((units, units), 1), own_row, 0.0), axis=1, keepdims=True
    )
    same = (mine_col == own_row) & (iota((units, units), 1) < iota((units, units), 0))
    slots[...] = jnp.sum(jnp.where(same, 1.0, 0.0), axis=1, keepdims=True)
    owners[...] = mine_col

    cot_y.wait_recv()
    cot_on.start()
    for copy in state_copies:
        copy.wait_recv()
    lane = iota((units, 128), 1).astype(jnp.float32)
    total_old = jnp.zeros((units, unit_rows), jnp.float32)
    for o in range(groups):
        hot = jnp.where((lane == slots[...]) & (owners[...] == o), 1.0, 0.0)
        total_old = total_old + lax.dot_general(
            hot, st_all[o], (((1,), (1,)), ((), ())), precision=HIGH, preferred_element_type=jnp.float32
        )
    old[...] = total_old

    def expand():
        return jnp.where(iota((slab, blocks), 0) // unit_rows == iota((slab, blocks), 1), 1.0, 0.0)

    def diagonal():
        return iota((slab, unit_rows), 0) % unit_rows == iota((slab, unit_rows), 1)

    def spread(t):
        wide = lax.dot_general(
            expand(),
            old[t * blocks : (t + 1) * blocks, :],
            (((1,), (0,)), ((), ())),
            precision=HIGH,
            preferred_element_type=jnp.float32,
        )
        factor[t] = jnp.sum(jnp.where(diagonal(), wide, 0.0), axis=1, keepdims=True)

    for t in range(groups // 2):
        spread(t)
    for copy in local[2:]:
        copy.wait()
    cot_core.wait_recv()
    cot_on.wait_recv()

    def rows(k):
        return pl.ds(k * step, step)

    def row_moments(t, k, squares):
        mean = jnp.sum(squares, axis=1, keepdims=True) / head + epsilon
        row = decay_rate * factor[t, rows(k), :] + (1.0 - decay_rate) * mean
        factor[t, rows(k), :] = lax.rsqrt(row)
        return row

    part_copies, z_copies, own_copies, forwards = {}, {}, {}, {}

    def multiply(k):
        for d in range(1, members):
            x_copies[k, d].wait_recv()
        gains = gain[:, rows(k)]
        total = jnp.zeros((step, cot.shape[1]), jnp.float32)
        for d in range(members):
            scaled = (x_all[d, :, rows(k)].astype(jnp.float32) * gains).astype(jnp.bfloat16)
            total = total + lax.dot_general(
                scaled,
                c_all[lax.rem(i + members - d, members)],
                (((0,), (0,)), ((), ())),
                preferred_element_type=jnp.float32,
            )
        total = total.astype(jnp.bfloat16)
        for t in range(groups):
            part[t // 2, t % 2, rows(k), :] = total[:, t * head : (t + 1) * head]
        part_copies[k] = remote(
            part.at[:, 1 - x, rows(k), :], x_recv.at[:, rows(k), :], ps.at[k], pr.at[k], (other_x, i)
        )
        part_copies[k].start()

    def pass_on(k):
        part_copies[k].wait_recv()
        for d in range(1, zn + 1):
            to = lax.rem(z + d, zn)
            both = part[to, x, rows(k), :].astype(jnp.float32) + x_recv[to, rows(k), :].astype(jnp.float32)
            if d == zn:
                grad[rows(k), :] = both
                continue
            z_send[d, rows(k), :] = both.astype(jnp.bfloat16)
            z_copies[k, d] = remote(
                z_send.at[d, rows(k), :], z_recv.at[d, rows(k), :], zs.at[k, d], zr.at[k, d], (z_peer(d), i)
            )
            z_copies[k, d].start()

    sums = []

    def finish(k):
        total = grad[rows(k), :]
        for d in range(1, zn):
            z_copies[k, d].wait_recv()
            total = total + z_recv[d, rows(k), :].astype(jnp.float32)
        total = total.astype(jnp.bfloat16)
        gathered[g, rows(k), :] = total
        mine = gathered.at[g, rows(k), :]
        for d in range(1, zn):
            own_copies[k, d] = remote(mine, mine, us.at[k, d], ur.at[k, d], (z_peer(d), i))
            own_copies[k, d].start()
        forwards[k, 0] = remote(mine, mine, fs.at[k, 0], fr.at[k, 0], (other_x, i))
        forwards[k, 0].start()
        squares = total.astype(jnp.float32) * total.astype(jnp.float32)
        row = row_moments(g, k, squares)
        rows_new[rows(k), :] = row
        sums.append(
            (jnp.sum(squares, axis=0, keepdims=True), jnp.sum(jnp.broadcast_to(row, squares.shape), axis=0, keepdims=True))
        )

    def absorb(t, k):
        value = gathered[t, rows(k), :].astype(jnp.float32)
        row_moments(t, k, value * value)

    def forward(k):
        for d in range(1, zn):
            t = lax.rem(z + zn - d, zn) * 2 + x
            own_copies[k, d].wait_recv()
            block = gathered.at[t, rows(k), :]
            forwards[k, d] = remote(block, block, fs.at[k, d], fr.at[k, d], (other_x, i))
            forwards[k, d].start()
        for d in range(1, zn):
            absorb(lax.rem(z + zn - d, zn) * 2 + x, k)

    def arrive(k):
        for d in range(zn):
            forwards[k, d].wait_recv()
            absorb(lax.rem(z + zn - d, zn) * 2 + 1 - x, k)

    stat_copies, note_copies = [], []

    def share_sums():
        stat[i, 0:1, :] = sum(s[0] for s in sums)
        stat[i, 1:2, :] = sum(s[1] for s in sums)
        for d in range(1, members):
            copy = remote(stat.at[i], stat.at[i], ts.at[d], tr.at[d], (g, intra_peer(d)))
            copy.start()
            stat_copies.append(copy)
        note[g, 0:unit_rows, 0:blocks] = lax.dot_general(
            jnp.where(diagonal(), rows_new[...], 0.0),
            expand(),
            (((0,), (0,)), ((), ())),
            precision=HIGH,
            preferred_element_type=jnp.float32,
        )

    def share_note():
        for copy in stat_copies:
            copy.wait_recv()
        col_total, row_total = stat[0, 0:1, :], stat[0, 1:2, :]
        for m in range(1, members):
            col_total = col_total + stat[m, 0:1, :]
            row_total = row_total + stat[m, 1:2, :]
        col_new = decay_rate * col_state[pl.ds(g, 1), :] + (1.0 - decay_rate) * (col_total / d_model + epsilon)
        note[g, unit_rows : unit_rows + 1, :] = col_new
        note[g, unit_rows + 1 : unit_rows + 2, :] = step_size * lax.rsqrt(col_new / (row_total / d_model))
        for d in range(1, groups):
            copy = remote(note.at[g], note.at[g], ns.at[d], nr.at[d], (grp_peer(d), i))
            copy.start()
            note_copies.append(copy)

    for k in range(CHUNKS + 4):
        if k < CHUNKS:
            multiply(k)
        if k < 2:
            spread(groups // 2 + 2 * k)
            spread(groups // 2 + 2 * k + 1)
        if 0 <= k - 1 < CHUNKS:
            pass_on(k - 1)
        if 0 <= k - 2 < CHUNKS:
            finish(k - 2)
            if k - 2 == CHUNKS - 1:
                share_sums()
        if 0 <= k - 3 < CHUNKS:
            forward(k - 3)
            if k - 3 == CHUNKS - 1:
                share_note()
        if 0 <= k - 4 < CHUNKS:
            arrive(k - 4)

    for copy in note_copies:
        copy.wait_recv()
    for t in range(groups):
        col_factor = note[t, unit_rows + 1 : unit_rows + 2, :]
        at = slice(t * head, (t + 1) * head)
        change = gathered[t].astype(jnp.float32) * factor[t] * col_factor
        out[:, at] = (w_all[:, at].astype(jnp.float32) - change).astype(jnp.bfloat16)

    got = jnp.zeros((unit_rows, 128), jnp.float32)
    hot = jnp.where((lane == slots[...]) & (owners[...] == g.astype(jnp.float32)), 1.0, 0.0)
    for t in range(groups):
        got = got + lax.dot_general(
            note[t, 0:unit_rows, 0:blocks],
            hot[t * blocks : (t + 1) * blocks],
            (((1,), (0,)), ((), ())),
            precision=HIGH,
            preferred_element_type=jnp.float32,
        )
        col_out[t : t + 1, :] = note[t, unit_rows : unit_rows + 1, :]
    row_out[...] = got[:, :capacity]

    sent = [cot_y, cot_core, cot_on, *x_copies.values(), *state_copies, *part_copies.values()]
    sent += [*z_copies.values(), *stat_copies, *note_copies, *own_copies.values(), *forwards.values()]
    for copy in sent:
        copy.wait_send()


def fused(normed, cotangent, norm_gain, weights, row_state, col_state, owner_table):
    groups = lax.axis_size("grp")
    members = lax.axis_size("intra")
    tokens, d_model = normed.shape
    slab, width = weights.shape
    tensors, head = col_state.shape
    capacity, unit_rows = row_state.shape[2:]
    units = owner_table.shape[0]
    zn = groups // 2
    bf16, f32 = jnp.bfloat16, jnp.float32
    vmem = pl.BlockSpec(memory_space=pltpu.VMEM)
    hbm = pl.BlockSpec(memory_space=pltpu.HBM)
    dma = pltpu.SemaphoreType.DMA
    note_rows = unit_rows + 8
    out, row_out, col_out = pl.pallas_call(
        functools.partial(kernel, d_model),
        out_shape=(
            jax.ShapeDtypeStruct((slab, width), bf16),
            jax.ShapeDtypeStruct((unit_rows, capacity), f32),
            jax.ShapeDtypeStruct((tensors, head), f32),
        ),
        in_specs=[hbm] * 7,
        out_specs=(vmem, vmem, vmem),
        scratch_shapes=[
            pltpu.VMEM((1, slab), f32),
            pltpu.VMEM((unit_rows, capacity), f32),
            pltpu.VMEM((tensors, head), f32),
            pltpu.VMEM((1, units), jnp.int32),
            pltpu.VMEM((members, tokens, slab), bf16),
            pltpu.VMEM((members, tokens, width), bf16),
            pltpu.VMEM((slab, width), bf16),
            pltpu.VMEM((groups, unit_rows, 128), f32),
            pltpu.VMEM((units, 1), f32),
            pltpu.VMEM((units, 1), f32),
            pltpu.VMEM((units, unit_rows), f32),
            pltpu.VMEM((tensors, slab, 1), f32),
            pltpu.VMEM((zn, 2, slab, head), bf16),
            pltpu.VMEM((zn, slab, head), bf16),
            pltpu.VMEM((zn, slab, head), bf16),
            pltpu.VMEM((zn, slab, head), bf16),
            pltpu.VMEM((slab, head), f32),
            pltpu.VMEM((slab, 1), f32),
            pltpu.VMEM((tensors, slab, head), bf16),
            pltpu.VMEM((members, 8, head), f32),
            pltpu.VMEM((groups, note_rows, 128), f32),
            dma((7,)),
            dma((3,)),
            dma((3,)),
            dma((CHUNKS, members)),
            dma((CHUNKS, members)),
            dma((groups,)),
            dma((groups,)),
            dma((CHUNKS,)),
            dma((CHUNKS,)),
            dma((CHUNKS, zn)),
            dma((CHUNKS, zn)),
            dma((members,)),
            dma((members,)),
            dma((groups,)),
            dma((groups,)),
            dma((CHUNKS, zn)),
            dma((CHUNKS, zn)),
            dma((CHUNKS, zn)),
            dma((CHUNKS, zn)),
        ],
        compiler_params=pltpu.CompilerParams(
            collective_id=0, has_side_effects=True, vmem_limit_bytes=48 * 2**20
        ),
        cost_estimate=pl.CostEstimate(
            flops=2 * members * tokens * slab * width, bytes_accessed=6 * 2**20, transcendentals=0
        ),
    )(
        normed,
        cotangent,
        norm_gain.reshape(1, d_model),
        weights,
        row_state[0, 0].T,
        col_state,
        owner_table.reshape(1, units),
    )
    return (out, row_out.T[None, None], col_out)


def solution(mesh):
    placed = (
        P(("grp", "intra"), None),
        P(("grp", "intra"), None),
        P(),
        P("intra", None),
        P("grp", "intra", None, None),
        P(),
        P(),
    )
    fits = mesh.shape["grp"] == 8 and mesh.shape["intra"] == 4
    return jax.shard_map(
        fused if fits else general,
        mesh=mesh,
        in_specs=placed,
        out_specs=(P("intra", None), P("grp", "intra", None, None), P()),
        check_vma=False,
    )
```

```python
import functools

import jax
import jax.numpy as jnp
from jax import lax
from jax.experimental import pallas as pl
from jax.experimental.pallas import tpu as pltpu
from jax.sharding import PartitionSpec as P

decay_rate = 0.8
step_size = 0.5
epsilon = 1e-06

MESH = pl.DeviceIdType.MESH
HIGH = lax.Precision.HIGHEST
CHUNKS = 8


def to_units(block, blocks, unit_rows, tensors, head):
    return (
        block.reshape(blocks, unit_rows, tensors, head)
        .transpose(2, 0, 1, 3)
        .reshape(tensors * blocks, unit_rows * head)
    )


def from_units(units, blocks, unit_rows, tensors, head):
    return (
        units.reshape(tensors, blocks, unit_rows, head)
        .transpose(1, 2, 0, 3)
        .reshape(blocks * unit_rows, tensors * head)
    )


def pick(hot, rows):
    return jnp.dot(hot.astype(jnp.bfloat16), rows, preferred_element_type=jnp.float32)


def general(normed, cotangent, norm_gain, weights, row_state, col_state, owner_table):
    groups = lax.axis_size("grp")
    members = lax.axis_size("intra")
    d_model = normed.shape[1]
    tokens_here = cotangent.shape[0]
    width = cotangent.shape[1]
    tensors = col_state.shape[0]
    head = col_state.shape[1]
    capacity = row_state.shape[2]
    unit_rows = row_state.shape[3]
    slab_rows = weights.shape[0]
    blocks = slab_rows // unit_rows
    unit_count = tensors * blocks
    scaled = (normed * norm_gain[None, :]).astype(jnp.bfloat16)
    columns = lax.all_to_all(scaled, "intra", split_axis=1, concat_axis=0, tiled=True)
    peer_grads = lax.all_gather(cotangent, "intra", axis=0, tiled=True)

    def add_term(total, pair):
        left, right = pair
        term = lax.dot_general(
            left, right, (((0,), (0,)), ((), ())), preferred_element_type=jnp.float32
        )
        return (total + term, None)

    slab, _ = lax.scan(
        add_term,
        jnp.zeros((slab_rows, width), jnp.float32),
        (
            columns.reshape(members, tokens_here, slab_rows),
            peer_grads.reshape(members, tokens_here, width),
        ),
    )
    owner_flat = owner_table[:, 0]
    owner_hot = owner_flat[:, None] == jnp.arange(groups, dtype=jnp.int32)[None, :]
    ids = jnp.arange(unit_count, dtype=jnp.int32)
    earlier = (owner_flat[:, None] == owner_flat[None, :]) & (ids[None, :] < ids[:, None])
    slot = jnp.sum(earlier.astype(jnp.int32), axis=1)
    place = owner_flat * capacity + slot
    hot = place[:, None] == jnp.arange(groups * capacity, dtype=jnp.int32)[None, :]
    my_group = lax.axis_index("grp")
    my_place = my_group * capacity + jnp.arange(capacity, dtype=jnp.int32)
    my_hot = my_place[:, None] == place[None, :]
    valid = jnp.any(my_hot, axis=1)
    weight_units = to_units(weights, blocks, unit_rows, tensors, head)
    grad_units = to_units(slab, blocks, unit_rows, tensors, head).astype(jnp.bfloat16)
    outgoing = pick(hot.T, grad_units).reshape(groups, capacity, unit_rows, head)
    incoming = lax.all_to_all(
        outgoing.astype(jnp.bfloat16), "grp", split_axis=0, concat_axis=0, tiled=True
    ).astype(jnp.float32)
    grad_own = jnp.sum(incoming, axis=0)
    own_weights = pick(my_hot, weight_units).reshape(capacity, unit_rows, head)
    unit_hot = (
        (ids // blocks)[:, None] == jnp.arange(tensors, dtype=jnp.int32)[None, :]
    ).astype(jnp.bfloat16)
    tensor_hot = pick(my_hot, unit_hot)
    squares = grad_own * grad_own
    row_mean = jnp.mean(squares, axis=2) + epsilon
    row_new = jnp.where(
        valid[:, None], decay_rate * row_state[0, 0] + (1.0 - decay_rate) * row_mean, 0.0
    )
    col_part = jnp.einsum("st,srh->th", tensor_hot, squares, precision=HIGH)
    row_part = jnp.einsum("st,sr->t", tensor_hot, row_new, precision=HIGH)
    col_total, row_total = lax.psum((col_part, row_part), ("grp", "intra"))
    col_new = decay_rate * col_state + (1.0 - decay_rate) * (col_total / d_model + epsilon)
    row_avg = row_total / d_model
    col_slot = jnp.dot(tensor_hot, col_new, precision=HIGH)
    avg_slot = jnp.where(valid, jnp.dot(tensor_hot, row_avg, precision=HIGH), 1.0)
    variance = row_new[:, :, None] * col_slot[:, None, :] / avg_slot[:, None, None]
    variance = jnp.where(valid[:, None, None], variance, 1.0)
    updated = (own_weights - step_size * grad_own / jnp.sqrt(variance)).astype(jnp.bfloat16)
    collected = lax.all_gather(updated, "grp", axis=0, tiled=True)
    mine = pick(hot, collected.reshape(groups * capacity, unit_rows * head)).astype(jnp.bfloat16)
    new_weights = from_units(mine, blocks, unit_rows, tensors, head)
    return (new_weights, row_new[None, None], col_new)


def iota(shape, axis):
    return lax.broadcasted_iota(jnp.int32, shape, axis)


def kernel(
    d_model,
    normed,
    cot,
    gain_in,
    weights,
    state_in,
    col_in,
    owner_in,
    out,
    row_out,
    col_out,
    gain,
    state,
    col_state,
    owner,
    x_all,
    c_all,
    w_all,
    st_all,
    slots,
    owners,
    old,
    factor,
    part,
    x_recv,
    z_send,
    z_recv,
    grad,
    rows_new,
    gathered,
    stat,
    note,
    local_sem,
    cs,
    cr,
    xs,
    xr,
    ss,
    sr,
    ps,
    pr,
    zs,
    zr,
    ts,
    tr,
    ns,
    nr,
    us,
    ur,
    fs,
    fr,
):
    groups = lax.axis_size("grp")
    members = lax.axis_size("intra")
    g = lax.axis_index("grp")
    i = lax.axis_index("intra")
    z, x = g // 2, g % 2
    zn = groups // 2
    slab = grad.shape[0]
    head = grad.shape[1]
    capacity, unit_rows = state.shape[1], state.shape[0]
    units = owner.shape[1]
    blocks = slab // unit_rows
    step = slab // CHUNKS
    other_core = i // 2 * 2 + (1 - i % 2)
    other_y = (1 - i // 2) * 2 + i % 2
    other_x = z * 2 + (1 - x)

    def grp_peer(d):
        return lax.rem(g + d, groups)

    def z_peer(d):
        return lax.rem(z + d, zn) * 2 + x

    def intra_peer(d):
        return lax.rem(i + d, members)

    def remote(src, dst, send, recv, to):
        return pltpu.make_async_remote_copy(
            src_ref=src, dst_ref=dst, send_sem=send, recv_sem=recv, device_id=to, device_id_type=MESH
        )

    barrier = pltpu.get_barrier_semaphore()
    for d in range(1, groups):
        pl.semaphore_signal(barrier, inc=1, device_id=(grp_peer(d), i), device_id_type=MESH)
    for d in range(1, members):
        pl.semaphore_signal(barrier, inc=1, device_id=(g, intra_peer(d)), device_id_type=MESH)

    slab_at = pl.ds(pl.multiple_of(i * slab, slab), slab)
    local = [
        pltpu.make_async_copy(state_in, state, local_sem.at[0]),
        pltpu.make_async_copy(owner_in, owner, local_sem.at[1]),
        pltpu.make_async_copy(cot, c_all.at[i], local_sem.at[2]),
        pltpu.make_async_copy(normed.at[:, slab_at], x_all.at[i], local_sem.at[3]),
        pltpu.make_async_copy(gain_in.at[:, slab_at], gain, local_sem.at[4]),
        pltpu.make_async_copy(col_in, col_state, local_sem.at[5]),
        pltpu.make_async_copy(weights, w_all, local_sem.at[6]),
    ]
    for copy in local:
        copy.start()
    st_all[g] = jnp.zeros_like(st_all[0])
    local[0].wait()
    st_all[g, :, :capacity] = state[...]
    pl.semaphore_wait(barrier, groups + members - 2)

    cot_y = remote(cot, c_all.at[i], cs.at[0], cr.at[0], (g, other_y))
    cot_core = remote(cot, c_all.at[i], cs.at[1], cr.at[1], (g, other_core))
    cot_on = remote(c_all.at[other_y], c_all.at[other_y], cs.at[2], cr.at[2], (g, other_core))
    cot_y.start()
    cot_core.start()
    x_copies = {}
    for k in range(CHUNKS):
        for d in range(1, members):
            to = intra_peer(d)
            x_copies[k, d] = remote(
                normed.at[:, pl.ds(pl.multiple_of(to * slab + k * step, step), step)],
                x_all.at[i, :, pl.ds(k * step, step)],
                xs.at[k, d],
                xr.at[k, d],
                (g, to),
            )
            x_copies[k, d].start()
    state_copies = []
    for d in range(1, groups):
        copy = remote(st_all.at[g], st_all.at[g], ss.at[d], sr.at[d], (grp_peer(d), i))
        copy.start()
        state_copies.append(copy)

    local[1].wait()
    own_row = owner[...].astype(jnp.float32)
    mine_col = jnp.sum(
        jnp.where(iota((units, units), 0) == iota((units, units), 1), own_row, 0.0), axis=1, keepdims=True
    )
    same = (mine_col == own_row) & (iota((units, units), 1) < iota((units, units), 0))
    slots[...] = jnp.sum(jnp.where(same, 1.0, 0.0), axis=1, keepdims=True)
    owners[...] = mine_col

    cot_y.wait_recv()
    cot_on.start()
    for copy in state_copies:
        copy.wait_recv()
    lane = iota((units, 128), 1).astype(jnp.float32)
    total_old = jnp.zeros((units, unit_rows), jnp.float32)
    for o in range(groups):
        hot = jnp.where((lane == slots[...]) & (owners[...] == o), 1.0, 0.0)
        total_old = total_old + lax.dot_general(
            hot, st_all[o], (((1,), (1,)), ((), ())), precision=HIGH, preferred_element_type=jnp.float32
        )
    old[...] = total_old

    def expand():
        return jnp.where(iota((slab, blocks), 0) // unit_rows == iota((slab, blocks), 1), 1.0, 0.0)

    def diagonal():
        return iota((slab, unit_rows), 0) % unit_rows == iota((slab, unit_rows), 1)

    def spread(t):
        wide = lax.dot_general(
            expand(),
            old[t * blocks : (t + 1) * blocks, :],
            (((1,), (0,)), ((), ())),
            precision=HIGH,
            preferred_element_type=jnp.float32,
        )
        factor[t] = jnp.sum(jnp.where(diagonal(), wide, 0.0), axis=1, keepdims=True)

    for t in range(groups // 2):
        spread(t)
    for copy in local[2:]:
        copy.wait()
    cot_core.wait_recv()
    cot_on.wait_recv()

    def rows(k):
        return pl.ds(k * step, step)

    def row_moments(t, k, squares):
        mean = jnp.sum(squares, axis=1, keepdims=True) / head + epsilon
        row = decay_rate * factor[t, rows(k), :] + (1.0 - decay_rate) * mean
        factor[t, rows(k), :] = lax.rsqrt(row)
        return row

    part_copies, z_copies, own_copies, forwards = {}, {}, {}, {}

    def multiply(k):
        for d in range(1, members):
            x_copies[k, d].wait_recv()
        gains = gain[:, rows(k)]
        depth = members * cot.shape[0]
        scaled = (x_all[:, :, rows(k)].reshape(depth, step).astype(jnp.float32) * gains).astype(jnp.bfloat16)
        total = lax.dot_general(
            scaled,
            c_all[...].reshape(depth, cot.shape[1]),
            (((0,), (0,)), ((), ())),
            preferred_element_type=jnp.float32,
        )
        total = total.astype(jnp.bfloat16)
        for t in range(groups):
            part[t // 2, t % 2, rows(k), :] = total[:, t * head : (t + 1) * head]
        part_copies[k] = remote(
            part.at[:, 1 - x, rows(k), :], x_recv.at[:, rows(k), :], ps.at[k], pr.at[k], (other_x, i)
        )
        part_copies[k].start()

    def pass_on(k):
        part_copies[k].wait_recv()
        for d in range(1, zn + 1):
            to = lax.rem(z + d, zn)
            both = part[to, x, rows(k), :].astype(jnp.float32) + x_recv[to, rows(k), :].astype(jnp.float32)
            if d == zn:
                grad[rows(k), :] = both
                continue
            z_send[d, rows(k), :] = both.astype(jnp.bfloat16)
            z_copies[k, d] = remote(
                z_send.at[d, rows(k), :], z_recv.at[d, rows(k), :], zs.at[k, d], zr.at[k, d], (z_peer(d), i)
            )
            z_copies[k, d].start()

    sums = []

    def finish(k):
        total = grad[rows(k), :]
        for d in range(1, zn):
            z_copies[k, d].wait_recv()
            total = total + z_recv[d, rows(k), :].astype(jnp.float32)
        total = total.astype(jnp.bfloat16)
        gathered[g, rows(k), :] = total
        mine = gathered.at[g, rows(k), :]
        for d in range(1, zn):
            own_copies[k, d] = remote(mine, mine, us.at[k, d], ur.at[k, d], (z_peer(d), i))
            own_copies[k, d].start()
        forwards[k, 0] = remote(mine, mine, fs.at[k, 0], fr.at[k, 0], (other_x, i))
        forwards[k, 0].start()
        squares = total.astype(jnp.float32) * total.astype(jnp.float32)
        row = row_moments(g, k, squares)
        rows_new[rows(k), :] = row
        sums.append(
            (jnp.sum(squares, axis=0, keepdims=True), jnp.sum(jnp.broadcast_to(row, squares.shape), axis=0, keepdims=True))
        )

    def absorb(t, k):
        value = gathered[t, rows(k), :].astype(jnp.float32)
        row_moments(t, k, value * value)

    def forward(k):
        for d in range(1, zn):
            t = lax.rem(z + zn - d, zn) * 2 + x
            own_copies[k, d].wait_recv()
            block = gathered.at[t, rows(k), :]
            forwards[k, d] = remote(block, block, fs.at[k, d], fr.at[k, d], (other_x, i))
            forwards[k, d].start()
        for d in range(1, zn):
            absorb(lax.rem(z + zn - d, zn) * 2 + x, k)

    def arrive(k):
        for d in range(zn):
            forwards[k, d].wait_recv()
            absorb(lax.rem(z + zn - d, zn) * 2 + 1 - x, k)

    stat_copies, note_copies = [], []

    def share_sums():
        stat[i, 0:1, :] = sum(s[0] for s in sums)
        stat[i, 1:2, :] = sum(s[1] for s in sums)
        for d in range(1, members):
            copy = remote(stat.at[i], stat.at[i], ts.at[d], tr.at[d], (g, intra_peer(d)))
            copy.start()
            stat_copies.append(copy)
        note[g, 0:unit_rows, 0:blocks] = lax.dot_general(
            jnp.where(diagonal(), rows_new[...], 0.0),
            expand(),
            (((0,), (0,)), ((), ())),
            precision=HIGH,
            preferred_element_type=jnp.float32,
        )

    def share_note():
        for copy in stat_copies:
            copy.wait_recv()
        col_total, row_total = stat[0, 0:1, :], stat[0, 1:2, :]
        for m in range(1, members):
            col_total = col_total + stat[m, 0:1, :]
            row_total = row_total + stat[m, 1:2, :]
        col_new = decay_rate * col_state[pl.ds(g, 1), :] + (1.0 - decay_rate) * (col_total / d_model + epsilon)
        note[g, unit_rows : unit_rows + 1, :] = col_new
        note[g, unit_rows + 1 : unit_rows + 2, :] = step_size * lax.rsqrt(col_new / (row_total / d_model))
        for d in range(1, groups):
            copy = remote(note.at[g], note.at[g], ns.at[d], nr.at[d], (grp_peer(d), i))
            copy.start()
            note_copies.append(copy)

    for k in range(CHUNKS + 4):
        if k < CHUNKS:
            multiply(k)
        if k < 2:
            spread(groups // 2 + 2 * k)
            spread(groups // 2 + 2 * k + 1)
        if 0 <= k - 1 < CHUNKS:
            pass_on(k - 1)
        if 0 <= k - 2 < CHUNKS:
            finish(k - 2)
            if k - 2 == CHUNKS - 1:
                share_sums()
        if 0 <= k - 3 < CHUNKS:
            forward(k - 3)
            if k - 3 == CHUNKS - 1:
                share_note()
        if 0 <= k - 4 < CHUNKS:
            arrive(k - 4)

    for copy in note_copies:
        copy.wait_recv()
    for t in range(groups):
        col_factor = note[t, unit_rows + 1 : unit_rows + 2, :]
        at = slice(t * head, (t + 1) * head)
        change = gathered[t].astype(jnp.float32) * factor[t] * col_factor
        out[:, at] = (w_all[:, at].astype(jnp.float32) - change).astype(jnp.bfloat16)

    got = jnp.zeros((unit_rows, 128), jnp.float32)
    hot = jnp.where((lane == slots[...]) & (owners[...] == g.astype(jnp.float32)), 1.0, 0.0)
    for t in range(groups):
        got = got + lax.dot_general(
            note[t, 0:unit_rows, 0:blocks],
            hot[t * blocks : (t + 1) * blocks],
            (((1,), (0,)), ((), ())),
            precision=HIGH,
            preferred_element_type=jnp.float32,
        )
        col_out[t : t + 1, :] = note[t, unit_rows : unit_rows + 1, :]
    row_out[...] = got[:, :capacity]

    sent = [cot_y, cot_core, cot_on, *x_copies.values(), *state_copies, *part_copies.values()]
    sent += [*z_copies.values(), *stat_copies, *note_copies, *own_copies.values(), *forwards.values()]
    for copy in sent:
        copy.wait_send()


def fused(normed, cotangent, norm_gain, weights, row_state, col_state, owner_table):
    groups = lax.axis_size("grp")
    members = lax.axis_size("intra")
    tokens, d_model = normed.shape
    slab, width = weights.shape
    tensors, head = col_state.shape
    capacity, unit_rows = row_state.shape[2:]
    units = owner_table.shape[0]
    zn = groups // 2
    bf16, f32 = jnp.bfloat16, jnp.float32
    vmem = pl.BlockSpec(memory_space=pltpu.VMEM)
    hbm = pl.BlockSpec(memory_space=pltpu.HBM)
    dma = pltpu.SemaphoreType.DMA
    note_rows = unit_rows + 8
    out, row_out, col_out = pl.pallas_call(
        functools.partial(kernel, d_model),
        out_shape=(
            jax.ShapeDtypeStruct((slab, width), bf16),
            jax.ShapeDtypeStruct((unit_rows, capacity), f32),
            jax.ShapeDtypeStruct((tensors, head), f32),
        ),
        in_specs=[hbm] * 7,
        out_specs=(vmem, vmem, vmem),
        scratch_shapes=[
            pltpu.VMEM((1, slab), f32),
            pltpu.VMEM((unit_rows, capacity), f32),
            pltpu.VMEM((tensors, head), f32),
            pltpu.VMEM((1, units), jnp.int32),
            pltpu.VMEM((members, tokens, slab), bf16),
            pltpu.VMEM((members, tokens, width), bf16),
            pltpu.VMEM((slab, width), bf16),
            pltpu.VMEM((groups, unit_rows, 128), f32),
            pltpu.VMEM((units, 1), f32),
            pltpu.VMEM((units, 1), f32),
            pltpu.VMEM((units, unit_rows), f32),
            pltpu.VMEM((tensors, slab, 1), f32),
            pltpu.VMEM((zn, 2, slab, head), bf16),
            pltpu.VMEM((zn, slab, head), bf16),
            pltpu.VMEM((zn, slab, head), bf16),
            pltpu.VMEM((zn, slab, head), bf16),
            pltpu.VMEM((slab, head), f32),
            pltpu.VMEM((slab, 1), f32),
            pltpu.VMEM((tensors, slab, head), bf16),
            pltpu.VMEM((members, 8, head), f32),
            pltpu.VMEM((groups, note_rows, 128), f32),
            dma((7,)),
            dma((3,)),
            dma((3,)),
            dma((CHUNKS, members)),
            dma((CHUNKS, members)),
            dma((groups,)),
            dma((groups,)),
            dma((CHUNKS,)),
            dma((CHUNKS,)),
            dma((CHUNKS, zn)),
            dma((CHUNKS, zn)),
            dma((members,)),
            dma((members,)),
            dma((groups,)),
            dma((groups,)),
            dma((CHUNKS, zn)),
            dma((CHUNKS, zn)),
            dma((CHUNKS, zn)),
            dma((CHUNKS, zn)),
        ],
        compiler_params=pltpu.CompilerParams(
            collective_id=0, has_side_effects=True, vmem_limit_bytes=62 * 2**20
        ),
        cost_estimate=pl.CostEstimate(
            flops=2 * members * tokens * slab * width, bytes_accessed=6 * 2**20, transcendentals=0
        ),
    )(
        normed,
        cotangent,
        norm_gain.reshape(1, d_model),
        weights,
        row_state[0, 0].T,
        col_state,
        owner_table.reshape(1, units),
    )
    return (out, row_out.T[None, None], col_out)


def solution(mesh):
    placed = (
        P(("grp", "intra"), None),
        P(("grp", "intra"), None),
        P(),
        P("intra", None),
        P("grp", "intra", None, None),
        P(),
        P(),
    )
    fits = mesh.shape["grp"] == 8 and mesh.shape["intra"] == 4
    return jax.shard_map(
        fused if fits else general,
        mesh=mesh,
        in_specs=placed,
        out_specs=(P("intra", None), P("grp", "intra", None, None), P()),
        check_vma=False,
    )
```
